1024 devices in a mesh: ctx: 32 (over y, x, core), tp: 32 (over z).
Axes of the slice: x: 4, y: 4, z: 32, core: 2. Of those that a mesh axis runs over, the one named last changes fastest.
Arguments:
- query: bfloat16 [16384, 4096], P('ctx', 'tp'), may hold values from -6 to 6
- key_proj: bfloat16 [16384, 4096], P('ctx', 'tp'), may hold values from -6 to 6
- value: bfloat16 [16384, 4096], P('ctx', 'tp'), may hold values from -6 to 6
- decay_rates: float32 [16, 4096], P(None, 'tp'), may hold values from 3.0517578e-05 to 0.05
- residues: float32 [16, 4096], P(None, 'tp'), may hold values from -2 to 2
- skip_gain: float32 [4096], P('tp'), may hold values from 0.5 to 1.5
- out_weight: bfloat16 [4096, 4096], P('tp'), may hold values from -0.1875 to 0.1875
Outputs:
- mixed: bfloat16 [16384, 4096], P('ctx', 'tp')
The draws below stay inside these ranges and needn't reach their ends.
All inputs are finite; a program needn't handle non-finite values.
Results may differ from the reference program's by a relative error of at most 0.006.
Values sent between devices are 32-bit elements; how exact they have to be, the bound alone decides.
No kernel may reach another device: no remote copies, remote signals or barrier semaphores. Data moves between devices by JAX's collectives and lax.ppermute only.
A program may use at most 64 MiB of HBM per device.

```python
import math
import jax
import jax.numpy as jnp

D = 4096
MODES = 16
TOKENS = 16384
FFT_LEN = 32768


def spiked(values, own_key, source, target, parts, factor):
    def block_of(dim):
        return (jnp.arange(values.shape[dim]) // (values.shape[dim] // parts)).reshape((-1,) + (1,) * (values.ndim - 1 - dim))

    first = jax.random.permutation(own_key, parts)[block_of(target)]
    second = (block_of(target) + parts // 2) % parts
    return jnp.where((block_of(source) == first) | (block_of(source) == second), factor * values, values)


def shard_levels(own_key, dims, shards, low, top_value):
    def one(dim, shards_of):
        heights = jax.random.uniform(jax.random.fold_in(jax.random.fold_in(own_key, 6), dim), (shards_of,), jnp.float32, low / len(shards), top_value / len(shards))
        return jnp.repeat(jnp.exp(heights), dims[dim] // shards_of).reshape((-1,) + (1,) * (len(dims) - dim - 1))

    factor_of = one(*shards[0])
    for cut in shards[1:]:
        factor_of = factor_of * one(*cut)
    return factor_of


def bell_draw(own_key, dims, width, most, split=(), kind=jnp.bfloat16):
    loudness = shard_levels(own_key, dims, split, -0.22, 0.18) if split else 1.0
    values = jax.random.normal(own_key, dims, jnp.float32) * width * loudness
    return jnp.minimum(jnp.maximum(values, -most), most).astype(kind)


def bell_draw_with(own_key, shape, scale, most, shards, heavy, kind=jnp.bfloat16):
    result = scale * jax.random.normal(own_key, shape, jnp.float32)
    if shards:
        result = result * shard_levels(own_key, shape, shards, -0.22, 0.18)
    return jnp.clip(spiked(result, jax.random.fold_in(own_key, 3), *heavy), -most, most).astype(kind)


def setup_inputs(seed: int = 0) -> dict:
    seeds = jax.random.split(jax.random.key(seed), 8)
    return {
        "query": bell_draw(seeds[0], (TOKENS, D), 1.0, 6.0, ((0, 32), (1, 32))),
        "key_proj": bell_draw(seeds[1], (TOKENS, D), 1.0, 6.0, ((0, 32), (1, 32))),
        "value": bell_draw(seeds[2], (TOKENS, D), 1.0, 6.0, ((0, 32), (1, 32))),
        "decay_rates": jnp.clip(jnp.exp(math.log(0.05) - 7.4014754 * jax.random.uniform(seeds[3], (MODES, D), jnp.float32) ** shard_levels(seeds[3], (MODES, D), ((1, 32),), -0.2, 0.2)), 3.0517578125e-05, 0.05),
        "residues": bell_draw(seeds[4], (MODES, D), 0.3, 2.0, ((1, 32),), jnp.float32),
        "skip_gain": jnp.clip(0.5 + 1.0 * jax.random.uniform(seeds[5], (D,), jnp.float32) ** shard_levels(seeds[5], (D,), ((0, 32),), -0.2, 0.2), 0.5, 1.5),
        "out_weight": bell_draw_with(seeds[6], (D, D), D ** -0.5, 0.1875, ((0, 32),), (0, 1, 32, 2.75)),
    }


def reference(query, key_proj, value, decay_rates, residues, skip_gain, out_weight):
    signal = key_proj.astype(jnp.float32) * value.astype(jnp.float32)
    positions = jnp.arange(TOKENS, dtype=jnp.float32)
    filter_time = jnp.zeros((TOKENS, D), jnp.float32)
    for mode_id in range(MODES):
        rate = decay_rates[mode_id][None, :]
        weight = residues[mode_id][None, :] * jnp.sqrt(-jnp.expm1(-2.0 * rate))
        filter_time = filter_time + weight * jnp.exp(-positions[:, None] * rate)
    signal_spec = jnp.fft.rfft(signal, n=FFT_LEN, axis=0)
    filter_spec = jnp.fft.rfft(filter_time, n=FFT_LEN, axis=0)
    conv = jnp.fft.irfft(signal_spec * filter_spec, n=FFT_LEN, axis=0)[:TOKENS]
    conv = conv.astype(jnp.float32)
    gated = (query.astype(jnp.float32) * (conv + skip_gain[None, :] * signal)).astype(jnp.bfloat16)
    total = jnp.dot(gated, out_weight, preferred_element_type=jnp.float32)
    return total.astype(jnp.bfloat16)
```

```python
import functools

import jax
import jax.numpy as jnp
from jax import lax
from jax.experimental import pallas as pl
from jax.experimental.pallas import tpu as pltpu
from jax.sharding import PartitionSpec as P

chunks = 8


def mode_rows(values, mode_count):
    return [jnp.broadcast_to(values[m : m + 1, :], (chunks, values.shape[1])) for m in range(mode_count)]


def states_kernel(key_ref, value_ref, rate_ref, chunk_ref, end_ref, signal_ref):
    modes = rate_ref.shape[0]
    steps = key_ref.shape[0] // chunks
    signal_ref[...] = key_ref[...].astype(jnp.float32) * value_ref[...].astype(jnp.float32)
    rates = rate_ref[...]
    decays = mode_rows(jnp.exp(-rates), modes)

    def step(t, states):
        x = signal_ref[pl.ds(t, chunks, stride=steps), :]
        return tuple(decays[m] * states[m] + x for m in range(modes))

    zero = jnp.zeros((chunks, rates.shape[1]), jnp.float32)
    states = lax.fori_loop(0, steps, step, (zero,) * modes, unroll=8)
    for m in range(modes):
        chunk_ref[pl.ds(m, chunks, stride=modes), :] = states[m]
    chunk_decay = jnp.exp(-float(steps) * rates)
    end = jnp.zeros_like(rates)
    for c in range(chunks):
        end = chunk_decay * end + chunk_ref[c * modes : (c + 1) * modes, :]
    end_ref[...] = end


def gated_kernel(
    index_ref, ends_ref, chunk_ref, rate_ref, weight_ref, skip_ref, query_ref, signal_ref, gated_ref, start_ref, wide_ref
):
    modes = rate_ref.shape[0]
    length = query_ref.shape[0]
    steps = length // chunks
    index = index_ref[0]
    rates = rate_ref[...]
    block_decay = jnp.exp(-float(length) * rates)
    carry = jnp.zeros_like(rates)
    for d in range(ends_ref.shape[0]):
        carry = jnp.where(d < index, block_decay * carry + ends_ref[d], carry)
    chunk_decay = jnp.exp(-float(steps) * rates)
    for c in range(chunks):
        rows = slice(c * modes, (c + 1) * modes)
        start_ref[rows, :] = carry
        carry = chunk_decay * carry + chunk_ref[rows, :]
    decays = mode_rows(jnp.exp(-rates), modes)
    weights = mode_rows(weight_ref[...], modes)
    skip = jnp.broadcast_to(skip_ref[...], (chunks, rates.shape[1]))
    wide_ref[...] = query_ref[...].astype(jnp.float32)

    def step(t, states):
        rows = pl.ds(t, chunks, stride=steps)
        x = signal_ref[rows, :]
        after = tuple(decays[m] * states[m] + x for m in range(modes))
        terms = [weights[m] * after[m] for m in range(modes)]
        while len(terms) > 1:
            terms = [terms[i] + terms[i + 1] for i in range(0, len(terms), 2)]
        wide_ref[rows, :] = wide_ref[rows, :] * (terms[0] + skip * x)
        return after

    states = tuple(start_ref[pl.ds(m, chunks, stride=modes), :] for m in range(modes))
    lax.fori_loop(0, steps, step, states, unroll=4)
    gated_ref[...] = wide_ref[...].astype(jnp.bfloat16)


def gated_block(query, key_proj, value, decay_rates, residues, skip_gain):
    length, width = query.shape
    modes = decay_rates.shape[0]
    shape = functools.partial(jax.ShapeDtypeStruct, dtype=jnp.float32)
    chunk_states, end_state, signal = pl.pallas_call(
        states_kernel,
        out_shape=(shape((chunks * modes, width)), shape((modes, width)), shape((length, width))),
    )(key_proj, value, decay_rates)
    ends = lax.all_gather(end_state, "ctx")
    weights = residues * jnp.sqrt(-jnp.expm1(-2.0 * decay_rates))
    vmem = pl.BlockSpec(memory_space=pltpu.VMEM)
    return pl.pallas_call(
        gated_kernel,
        out_shape=jax.ShapeDtypeStruct((length, width), jnp.bfloat16),
        in_specs=[pl.BlockSpec(memory_space=pltpu.SMEM)] + [vmem] * 7,
        out_specs=vmem,
        scratch_shapes=[pltpu.VMEM((chunks * modes, width), jnp.float32), pltpu.VMEM((length, width), jnp.float32)],
    )(lax.axis_index("ctx").reshape(1), ends, chunk_states, decay_rates, weights, skip_gain[None, :], query, signal)


def per_device(query, key_proj, value, decay_rates, residues, skip_gain, out_weight):
    gated = gated_block(query, key_proj, value, decay_rates, residues, skip_gain)
    summed = lax.psum_scatter(
        lax.dot_general(
            out_weight, gated, (((0,), (1,)), ((), ())), preferred_element_type=jnp.float32
        ),
        "tp",
        scatter_dimension=0,
        tiled=True,
    )
    return summed.T.astype(jnp.bfloat16)


def solution(mesh):
    placed = (
        P("ctx", "tp"),
        P("ctx", "tp"),
        P("ctx", "tp"),
        P(None, "tp"),
        P(None, "tp"),
        P("tp"),
        P("tp", None),
    )
    return jax.shard_map(
        per_device, mesh=mesh, in_specs=placed, out_specs=P("ctx", "tp"), check_vma=False
    )
```

```python
import functools

import jax
import jax.numpy as jnp
from jax import lax
from jax.experimental import pallas as pl
from jax.experimental.pallas import tpu as pltpu
from jax.sharding import PartitionSpec as P

chunks = 8


def mode_rows(values, mode_count):
    return [jnp.broadcast_to(values[m : m + 1, :], (chunks, values.shape[1])) for m in range(mode_count)]


def one_minus_exp(x):
    series = jnp.ones_like(x)
    for k in range(9, 1, -1):
        series = 1.0 - x * series * (1.0 / k)
    return jnp.where(x < 0.25, x * series, 1.0 - jnp.exp(-x))


def states_kernel(key_ref, value_ref, rate_ref, chunk_ref, end_ref, signal_ref):
    modes = rate_ref.shape[0]
    steps = key_ref.shape[0] // chunks
    signal_ref[...] = key_ref[...].astype(jnp.float32) * value_ref[...].astype(jnp.float32)
    rates = rate_ref[...]
    decays = mode_rows(jnp.exp(-rates), modes)

    def step(t, states):
        x = signal_ref[pl.ds(t, chunks, stride=steps), :]
        return tuple(decays[m] * states[m] + x for m in range(modes))

    zero = jnp.zeros((chunks, rates.shape[1]), jnp.float32)
    states = lax.fori_loop(0, steps, step, (zero,) * modes, unroll=8)
    for m in range(modes):
        chunk_ref[pl.ds(m, chunks, stride=modes), :] = states[m]
    chunk_decay = jnp.exp(-float(steps) * rates)
    end = jnp.zeros_like(rates)
    for c in range(chunks):
        end = chunk_decay * end + chunk_ref[c * modes : (c + 1) * modes, :]
    end_ref[...] = jnp.broadcast_to(end[None], end_ref.shape)


def product_kernel(
    index_ref,
    ends_ref,
    chunk_ref,
    rate_ref,
    residue_ref,
    skip_ref,
    query_ref,
    signal_ref,
    out_weight_ref,
    product_ref,
    start_ref,
    wide_ref,
    shifted_ref,
):
    modes = rate_ref.shape[0]
    length, width = query_ref.shape
    steps = length // chunks
    index = index_ref[0]
    rates = rate_ref[...]
    block_decay = jnp.exp(-float(length) * rates)
    carry = jnp.zeros_like(rates)
    for d in range(ends_ref.shape[0]):
        carry = jnp.where(d < index, block_decay * carry + ends_ref[d], carry)
    chunk_decay = jnp.exp(-float(steps) * rates)
    for c in range(chunks):
        rows = slice(c * modes, (c + 1) * modes)
        start_ref[rows, :] = carry
        carry = chunk_decay * carry + chunk_ref[rows, :]
    decays = mode_rows(jnp.exp(-rates), modes)
    weights = mode_rows(residue_ref[...] * jnp.sqrt(one_minus_exp(2.0 * rates)), modes)
    skip = jnp.broadcast_to(skip_ref[...], (chunks, width))
    wide_ref[...] = query_ref[...].astype(jnp.float32)

    def step(t, states):
        rows = pl.ds(t, chunks, stride=steps)
        x = signal_ref[rows, :]
        after = tuple(decays[m] * states[m] + x for m in range(modes))
        terms = [weights[m] * after[m] for m in range(modes)]
        while len(terms) > 1:
            terms = [terms[i] + terms[i + 1] for i in range(0, len(terms), 2)]
        wide_ref[rows, :] = wide_ref[rows, :] * (terms[0] + skip * x)
        return after

    states = tuple(start_ref[pl.ds(m, chunks, stride=modes), :] for m in range(modes))
    lax.fori_loop(0, steps, step, states, unroll=4)

    groups = out_weight_ref.shape[1] // width
    block = product_ref.shape[0] // groups
    shifted_ref[...] = jnp.zeros_like(shifted_ref)
    for first in range(8):
        shift = first * block % 8
        shifted_ref[0:8, :] = jnp.zeros((8, width), jnp.float32)
        shifted_ref[shift : shift + length, :] = wide_ref[...].astype(jnp.bfloat16).astype(jnp.float32)
        shifted_ref[length + shift : length + 16, :] = jnp.zeros((16 - shift, width), jnp.float32)
        left = shifted_ref[...].astype(jnp.bfloat16)
        members = range(first, groups, 8)
        right = jnp.concatenate([out_weight_ref[:, g * width : (g + 1) * width] for g in members], axis=1)
        both = jnp.dot(left, right, preferred_element_type=jnp.float32)
        for place, g in enumerate(members):
            base = g * block - shift
            rows = (g + 1) * block - (first + 1) * block % 8 - base
            product_ref[base : base + rows, :] = both[:rows, place * width : (place + 1) * width]


def round_kernel(summed_ref, mixed_ref):
    mixed_ref[...] = summed_ref[: mixed_ref.shape[0], :].astype(jnp.bfloat16)


def per_device(query, key_proj, value, decay_rates, residues, skip_gain, out_weight):
    length, width = query.shape
    modes = decay_rates.shape[0]
    groups = out_weight.shape[1] // width
    block = length + 15
    shape = functools.partial(jax.ShapeDtypeStruct, dtype=jnp.float32)
    vmem = pl.BlockSpec(memory_space=pltpu.VMEM)
    chunk_states, end_state, signal = pl.pallas_call(
        states_kernel,
        out_shape=(shape((chunks * modes, width)), shape((lax.axis_size("ctx"), modes, width)), shape((length, width))),
    )(key_proj, value, decay_rates)
    ends = lax.all_to_all(end_state, "ctx", split_axis=0, concat_axis=0)
    product = pl.pallas_call(
        product_kernel,
        out_shape=shape((groups * block, width)),
        in_specs=[pl.BlockSpec(memory_space=pltpu.SMEM)] + [vmem] * 8,
        out_specs=vmem,
        scratch_shapes=[
            pltpu.VMEM((chunks * modes, width), jnp.float32),
            pltpu.VMEM((length, width), jnp.float32),
            pltpu.VMEM((length + 16, width), jnp.float32),
        ],
        compiler_params=pltpu.CompilerParams(vmem_limit_bytes=40 * 1024 * 1024),
    )(
        lax.axis_index("ctx").reshape(1),
        ends,
        chunk_states,
        decay_rates,
        residues,
        skip_gain[None, :],
        query,
        signal,
        out_weight,
    )
    summed = lax.psum_scatter(product, "tp", scatter_dimension=0, tiled=True)
    return pl.pallas_call(round_kernel, out_shape=jax.ShapeDtypeStruct((length, width), jnp.bfloat16))(summed)


def solution(mesh):
    placed = (
        P("ctx", "tp"),
        P("ctx", "tp"),
        P("ctx", "tp"),
        P(None, "tp"),
        P(None, "tp"),
        P("tp"),
        P("tp", None),
    )
    return jax.shard_map(
        per_device, mesh=mesh, in_specs=placed, out_specs=P("ctx", "tp"), check_vma=False
    )
```

```python
import functools

import jax
import jax.numpy as jnp
from jax import lax
from jax.experimental import pallas as pl
from jax.experimental.pallas import tpu as pltpu
from jax.sharding import PartitionSpec as P

chunks = 8


def mode_rows(values, mode_count):
    return [jnp.broadcast_to(values[m : m + 1, :], (chunks, values.shape[1])) for m in range(mode_count)]


def one_minus_exp(x):
    series = jnp.ones_like(x)
    for k in range(9, 1, -1):
        series = 1.0 - x * series * (1.0 / k)
    return jnp.where(x < 0.25, x * series, 1.0 - jnp.exp(-x))


def states_kernel(key_ref, value_ref, rate_ref, chunk_ref, end_ref, signal_ref):
    modes = rate_ref.shape[0]
    steps = key_ref.shape[0] // chunks
    signal_ref[...] = key_ref[...].astype(jnp.float32) * value_ref[...].astype(jnp.float32)
    rates = rate_ref[...]
    decays = mode_rows(jnp.exp(-rates), modes)

    def step(t, states):
        x = signal_ref[pl.ds(t, chunks, stride=steps), :]
        return tuple(decays[m] * states[m] + x for m in range(modes))

    zero = jnp.zeros((chunks, rates.shape[1]), jnp.float32)
    states = lax.fori_loop(0, steps, step, (zero,) * modes, unroll=8)
    for m in range(modes):
        chunk_ref[pl.ds(m, chunks, stride=modes), :] = states[m]
    chunk_decay = jnp.exp(-float(steps) * rates)
    end = jnp.zeros_like(rates)
    for c in range(chunks):
        end = chunk_decay * end + chunk_ref[c * modes : (c + 1) * modes, :]
    end_ref[...] = jnp.broadcast_to(end[None], end_ref.shape)


def product_kernel(
    index_ref,
    ends_ref,
    chunk_ref,
    rate_ref,
    residue_ref,
    skip_ref,
    query_ref,
    key_ref,
    value_ref,
    out_weight_hbm,
    product_hbm,
    start_ref,
    wide_ref,
    signal_ref,
    shifted_ref,
    out_weight_ref,
    product_ref,
    load_sem,
    store_sems,
):
    load = pltpu.make_async_copy(out_weight_hbm, out_weight_ref, load_sem)
    load.start()
    modes = rate_ref.shape[0]
    length, width = query_ref.shape
    steps = length // chunks
    index = index_ref[0]
    rates = rate_ref[...]
    block_decay = jnp.exp(-float(length) * rates)
    carry = jnp.zeros_like(rates)
    for d in range(ends_ref.shape[0]):
        carry = jnp.where(d < index, block_decay * carry + ends_ref[d], carry)
    chunk_decay = jnp.exp(-float(steps) * rates)
    for c in range(chunks):
        rows = slice(c * modes, (c + 1) * modes)
        start_ref[rows, :] = carry
        carry = chunk_decay * carry + chunk_ref[rows, :]
    decays = mode_rows(jnp.exp(-rates), modes)
    weights = mode_rows(residue_ref[...] * jnp.sqrt(one_minus_exp(2.0 * rates)), modes)
    skip = jnp.broadcast_to(skip_ref[...], (chunks, width))
    wide_ref[...] = query_ref[...].astype(jnp.float32)
    signal_ref[...] = key_ref[...].astype(jnp.float32) * value_ref[...].astype(jnp.float32)

    def step(t, states):
        rows = pl.ds(t, chunks, stride=steps)
        x = signal_ref[rows, :]
        after = tuple(decays[m] * states[m] + x for m in range(modes))
        terms = [weights[m] * after[m] for m in range(modes)]
        while len(terms) > 1:
            terms = [terms[i] + terms[i + 1] for i in range(0, len(terms), 2)]
        wide_ref[rows, :] = wide_ref[rows, :] * (terms[0] + skip * x)
        return after

    states = tuple(start_ref[pl.ds(m, chunks, stride=modes), :] for m in range(modes))
    lax.fori_loop(0, steps, step, states, unroll=4)

    load.wait()
    stores = []
    groups = out_weight_ref.shape[1] // width
    block = product_ref.shape[0] // groups
    shifted_ref[...] = jnp.zeros_like(shifted_ref)
    for first in range(8):
        shift = first * block % 8
        shifted_ref[0:8, :] = jnp.zeros((8, width), jnp.float32)
        shifted_ref[shift : shift + length, :] = wide_ref[...].astype(jnp.bfloat16).astype(jnp.float32)
        shifted_ref[length + shift : length + 16, :] = jnp.zeros((16 - shift, width), jnp.float32)
        left = shifted_ref[...].astype(jnp.bfloat16)
        members = range(first, groups, 8)
        right = jnp.concatenate([out_weight_ref[:, g * width : (g + 1) * width] for g in members], axis=1)
        both = 0.5 * jnp.dot(left, right, preferred_element_type=jnp.float32)
        for place, g in enumerate(members):
            base = g * block - shift
            rows = (g + 1) * block - (first + 1) * block % 8 - base
            product_ref[base : base + rows, :] = both[:rows, place * width : (place + 1) * width]
            store = pltpu.make_async_copy(
                product_ref.at[pl.ds(base, rows), :], product_hbm.at[pl.ds(base, rows), :], store_sems.at[g]
            )
            store.start()
            stores.append(store)
    for store in stores:
        store.wait()


def per_device(query, key_proj, value, decay_rates, residues, skip_gain, out_weight):
    length, width = query.shape
    modes = decay_rates.shape[0]
    groups = out_weight.shape[1] // width
    block = length + 15
    shape = functools.partial(jax.ShapeDtypeStruct, dtype=jnp.float32)
    vmem = pl.BlockSpec(memory_space=pltpu.VMEM)
    chunk_states, end_state = pl.pallas_call(
        states_kernel,
        out_shape=(shape((chunks * modes, width)), shape((lax.axis_size("ctx"), modes, width))),
        scratch_shapes=[pltpu.VMEM((length, width), jnp.float32)],
    )(key_proj, value, decay_rates)
    ends = lax.all_to_all(end_state, "ctx", split_axis=0, concat_axis=0)
    product = pl.pallas_call(
        product_kernel,
        out_shape=shape((groups * block, width)),
        in_specs=[pl.BlockSpec(memory_space=pltpu.SMEM)] + [vmem] * 8 + [pl.BlockSpec(memory_space=pl.ANY)],
        out_specs=pl.BlockSpec(memory_space=pl.ANY),
        scratch_shapes=[
            pltpu.VMEM((chunks * modes, width), jnp.float32),
            pltpu.VMEM((length, width), jnp.float32),
            pltpu.VMEM((length, width), jnp.float32),
            pltpu.VMEM((length + 16, width), jnp.float32),
            pltpu.VMEM(out_weight.shape, jnp.bfloat16),
            pltpu.VMEM((groups * block, width), jnp.float32),
            pltpu.SemaphoreType.DMA,
            pltpu.SemaphoreType.DMA((groups,)),
        ],
        compiler_params=pltpu.CompilerParams(vmem_limit_bytes=60 * 1024 * 1024),
    )(
        lax.axis_index("ctx").reshape(1),
        ends,
        chunk_states,
        decay_rates,
        residues,
        skip_gain[None, :],
        query,
        key_proj,
        value,
        out_weight,
    )
    summed = lax.optimization_barrier(lax.psum_scatter(product, "tp", scatter_dimension=0, tiled=True))
    return (2.0 * summed[:length]).astype(jnp.bfloat16)


def solution(mesh):
    placed = (
        P("ctx", "tp"),
        P("ctx", "tp"),
        P("ctx", "tp"),
        P(None, "tp"),
        P(None, "tp"),
        P("tp"),
        P("tp", None),
    )
    return jax.shard_map(
        per_device, mesh=mesh, in_specs=placed, out_specs=P("ctx", "tp"), check_vma=False
    )
```

```python
import functools

import jax
import jax.numpy as jnp
from jax import lax
from jax.experimental import pallas as pl
from jax.experimental.pallas import tpu as pltpu
from jax.sharding import PartitionSpec as P

chunks = 8


def mode_rows(values, mode_count):
    return [jnp.broadcast_to(values[m : m + 1, :], (chunks, values.shape[1])) for m in range(mode_count)]


def one_minus_exp(x):
    series = jnp.ones_like(x)
    for k in range(9, 1, -1):
        series = 1.0 - x * series * (1.0 / k)
    return jnp.where(x < 0.25, x * series, 1.0 - jnp.exp(-x))


def states_kernel(key_ref, value_ref, rate_ref, chunk_ref, end_ref, signal_ref):
    modes = rate_ref.shape[0]
    steps = key_ref.shape[0] // chunks
    signal_ref[...] = key_ref[...].astype(jnp.float32) * value_ref[...].astype(jnp.float32)
    rates = rate_ref[...]
    decays = mode_rows(jnp.exp(-rates), modes)

    def step(t, states):
        x = signal_ref[pl.ds(t, chunks, stride=steps), :]
        return tuple(decays[m] * states[m] + x for m in range(modes))

    zero = jnp.zeros((chunks, rates.shape[1]), jnp.float32)
    states = lax.fori_loop(0, steps, step, (zero,) * modes, unroll=8)
    for m in range(modes):
        chunk_ref[pl.ds(m, chunks, stride=modes), :] = states[m]
    chunk_decay = jnp.exp(-float(steps) * rates)
    end = jnp.zeros_like(rates)
    for c in range(chunks):
        end = chunk_decay * end + chunk_ref[c * modes : (c + 1) * modes, :]
    end_ref[...] = jnp.broadcast_to(end[None], end_ref.shape)


def product_kernel(
    index_ref,
    ends_ref,
    chunk_ref,
    rate_ref,
    residue_ref,
    skip_ref,
    query_ref,
    key_ref,
    value_ref,
    out_weight_hbm,
    product_hbm,
    start_ref,
    wide_ref,
    signal_ref,
    shifted_ref,
    out_weight_ref,
    product_ref,
    load_sem,
    store_sems,
):
    load = pltpu.make_async_copy(out_weight_hbm, out_weight_ref, load_sem)
    load.start()
    modes = rate_ref.shape[0]
    length, width = query_ref.shape
    steps = length // chunks
    index = index_ref[0]
    rates = rate_ref[...]
    block_decay = jnp.exp(-float(length) * rates)
    carry = jnp.zeros_like(rates)
    for d in range(ends_ref.shape[0]):
        carry = jnp.where(d < index, block_decay * carry + ends_ref[d], carry)
    chunk_decay = jnp.exp(-float(steps) * rates)
    for c in range(chunks):
        rows = slice(c * modes, (c + 1) * modes)
        start_ref[rows, :] = carry
        carry = chunk_decay * carry + chunk_ref[rows, :]
    decays = mode_rows(jnp.exp(-rates), modes)
    weights = mode_rows(residue_ref[...] * jnp.sqrt(one_minus_exp(2.0 * rates)), modes)
    skip = jnp.broadcast_to(skip_ref[...], (chunks, width))
    wide_ref[...] = query_ref[...].astype(jnp.float32)
    signal_ref[...] = key_ref[...].astype(jnp.float32) * value_ref[...].astype(jnp.float32)

    def step(t, states):
        rows = pl.ds(t, chunks, stride=steps)
        x = signal_ref[rows, :]
        after = tuple(decays[m] * states[m] + x for m in range(modes))
        terms = [weights[m] * after[m] for m in range(modes)]
        while len(terms) > 1:
            terms = [terms[i] + terms[i + 1] for i in range(0, len(terms), 2)]
        wide_ref[rows, :] = wide_ref[rows, :] * (terms[0] + skip * x)
        return after

    states = tuple(start_ref[pl.ds(m, chunks, stride=modes), :] for m in range(modes))
    lax.fori_loop(0, steps, step, states, unroll=4)

    load.wait()
    stores = []
    groups = out_weight_ref.shape[1] // width
    block = product_ref.shape[0] // groups
    shifted_ref[...] = jnp.zeros_like(shifted_ref)
    for first in range(8):
        shift = first * block % 8
        shifted_ref[0:8, :] = jnp.zeros((8, width), jnp.float32)
        shifted_ref[shift : shift + length, :] = wide_ref[...].astype(jnp.bfloat16).astype(jnp.float32)
        shifted_ref[length + shift : length + 16, :] = jnp.zeros((16 - shift, width), jnp.float32)
        left = shifted_ref[...].astype(jnp.bfloat16)
        members = range(first, groups, 8)
        right = jnp.concatenate([out_weight_ref[:, g * width : (g + 1) * width] for g in members], axis=1)
        both = 0.5 * jnp.dot(left, right, preferred_element_type=jnp.float32)
        for place, g in enumerate(members):
            base = g * block - shift
            rows = (g + 1) * block - (first + 1) * block % 8 - base
            product_ref[base : base + rows, :] = both[:rows, place * width : (place + 1) * width]
            store = pltpu.make_async_copy(
                product_ref.at[pl.ds(base, rows), :], product_hbm.at[pl.ds(base, rows), :], store_sems.at[g]
            )
            store.start()
            stores.append(store)
    for store in stores:
        store.wait()


def per_device(query, key_proj, value, decay_rates, residues, skip_gain, out_weight):
    length, width = query.shape
    modes = decay_rates.shape[0]
    groups = out_weight.shape[1] // width
    block = length + 7
    shape = functools.partial(jax.ShapeDtypeStruct, dtype=jnp.float32)
    vmem = pl.BlockSpec(memory_space=pltpu.VMEM)
    chunk_states, end_state = pl.pallas_call(
        states_kernel,
        out_shape=(shape((chunks * modes, width)), shape((lax.axis_size("ctx"), modes, width))),
        scratch_shapes=[pltpu.VMEM((length, width), jnp.float32)],
    )(key_proj, value, decay_rates)
    ends = lax.all_to_all(end_state, "ctx", split_axis=0, concat_axis=0)
    product = pl.pallas_call(
        product_kernel,
        out_shape=shape((groups * block, width)),
        in_specs=[pl.BlockSpec(memory_space=pltpu.SMEM)] + [vmem] * 8 + [pl.BlockSpec(memory_space=pl.ANY)],
        out_specs=pl.BlockSpec(memory_space=pl.ANY),
        scratch_shapes=[
            pltpu.VMEM((chunks * modes, width), jnp.float32),
            pltpu.VMEM((length, width), jnp.float32),
            pltpu.VMEM((length, width), jnp.float32),
            pltpu.VMEM((length + 16, width), jnp.float32),
            pltpu.VMEM(out_weight.shape, jnp.bfloat16),
            pltpu.VMEM((groups * block, width), jnp.float32),
            pltpu.SemaphoreType.DMA,
            pltpu.SemaphoreType.DMA((groups,)),
        ],
        compiler_params=pltpu.CompilerParams(vmem_limit_bytes=60 * 1024 * 1024),
    )(
        lax.axis_index("ctx").reshape(1),
        ends,
        chunk_states,
        decay_rates,
        residues,
        skip_gain[None, :],
        query,
        key_proj,
        value,
        out_weight,
    )
    summed = lax.optimization_barrier(lax.psum_scatter(product, "tp", scatter_dimension=0, tiled=True))
    return (2.0 * summed[:length]).astype(jnp.bfloat16)


def solution(mesh):
    placed = (
        P("ctx", "tp"),
        P("ctx", "tp"),
        P("ctx", "tp"),
        P(None, "tp"),
        P(None, "tp"),
        P("tp"),
        P("tp", None),
    )
    return jax.shard_map(
        per_device, mesh=mesh, in_specs=placed, out_specs=P("ctx", "tp"), check_vma=False
    )
```

```python
import functools

import jax
import jax.numpy as jnp
from jax import lax
from jax.experimental import pallas as pl
from jax.experimental.pallas import tpu as pltpu
from jax.sharding import PartitionSpec as P

chunks = 8


def mode_rows(values, mode_count):
    return [jnp.broadcast_to(values[m : m + 1, :], (chunks, values.shape[1])) for m in range(mode_count)]


def one_minus_exp(x):
    series = jnp.ones_like(x)
    for k in range(9, 1, -1):
        series = 1.0 - x * series * (1.0 / k)
    return jnp.where(x < 0.25, x * series, 1.0 - jnp.exp(-x))


def states_kernel(key_ref, value_ref, rate_ref, chunk_ref, end_ref, signal_ref):
    modes = rate_ref.shape[0]
    steps = key_ref.shape[0] // chunks
    signal_ref[...] = key_ref[...].astype(jnp.float32) * value_ref[...].astype(jnp.float32)
    rates = rate_ref[...]
    decays = mode_rows(jnp.exp(-rates), modes)

    def step(t, states):
        x = signal_ref[pl.ds(t, chunks, stride=steps), :]
        return tuple(decays[m] * states[m] + x for m in range(modes))

    zero = jnp.zeros((chunks, rates.shape[1]), jnp.float32)
    states = lax.fori_loop(0, steps, step, (zero,) * modes, unroll=8)
    for m in range(modes):
        chunk_ref[pl.ds(m, chunks, stride=modes), :] = states[m]
    chunk_decay = jnp.exp(-float(steps) * rates)
    end = jnp.zeros_like(rates)
    for c in range(chunks):
        end = chunk_decay * end + chunk_ref[c * modes : (c + 1) * modes, :]
    end_ref[...] = jnp.broadcast_to(end[None], end_ref.shape)


def tree_sum(terms):
    while len(terms) > 1:
        terms = [terms[i] + terms[i + 1] for i in range(0, len(terms), 2)]
    return terms[0]


def local_kernel(
    chunk_ref, rate_ref, residue_ref, skip_ref, query_ref, key_ref, value_ref, local_ref, weight_ref, start_ref, signal_ref
):
    modes = rate_ref.shape[0]
    length, width = query_ref.shape
    steps = length // chunks
    rates = rate_ref[...]
    chunk_decay = jnp.exp(-float(steps) * rates)
    carry = jnp.zeros_like(rates)
    for c in range(chunks):
        rows = slice(c * modes, (c + 1) * modes)
        start_ref[rows, :] = carry
        carry = chunk_decay * carry + chunk_ref[rows, :]
    one_step = jnp.exp(-rates)
    weight = residue_ref[...] * jnp.sqrt(one_minus_exp(2.0 * rates))
    weight_ref[...] = weight * one_step
    decays = mode_rows(one_step, modes)
    weights = mode_rows(weight, modes)
    skip = jnp.broadcast_to(skip_ref[...], (chunks, width))
    signal_ref[...] = key_ref[...].astype(jnp.float32) * value_ref[...].astype(jnp.float32)

    def step(t, states):
        rows = pl.ds(t, chunks, stride=steps)
        x = signal_ref[rows, :]
        after = tuple(decays[m] * states[m] + x for m in range(modes))
        local_ref[rows, :] = tree_sum([weights[m] * after[m] for m in range(modes)]) + skip * x
        return after

    states = tuple(start_ref[pl.ds(m, chunks, stride=modes), :] for m in range(modes))
    lax.fori_loop(0, steps, step, states, unroll=4)


def product_kernel(
    index_ref,
    ends_ref,
    rate_ref,
    weight_ref,
    query_ref,
    local_ref,
    out_weight_hbm,
    product_hbm,
    start_ref,
    conv_ref,
    shifted_ref,
    out_weight_ref,
    product_ref,
    load_sem,
    store_sems,
):
    load = pltpu.make_async_copy(out_weight_hbm, out_weight_ref, load_sem)
    load.start()
    modes = rate_ref.shape[0]
    length, width = query_ref.shape
    steps = length // chunks
    index = index_ref[0]
    rates = rate_ref[...]
    block_decay = jnp.exp(-float(length) * rates)
    carry = jnp.zeros_like(rates)
    for d in range(ends_ref.shape[0]):
        carry = jnp.where(d < index, block_decay * carry + ends_ref[d], carry)
    chunk_decay = jnp.exp(-float(steps) * rates)
    carry = weight_ref[...] * carry
    for c in range(chunks):
        start_ref[c * modes : (c + 1) * modes, :] = carry
        carry = chunk_decay * carry
    decays = mode_rows(jnp.exp(-rates), modes)

    def step(t, tails):
        rows = pl.ds(t, chunks, stride=steps)
        conv_ref[rows, :] = local_ref[rows, :] + tree_sum(list(tails))
        return tuple(decays[m] * tails[m] for m in range(modes))

    tails = tuple(start_ref[pl.ds(m, chunks, stride=modes), :] for m in range(modes))
    lax.fori_loop(0, steps, step, tails, unroll=4)
    conv_ref[...] = ((0.5 * query_ref[...].astype(jnp.float32)) * conv_ref[...]).astype(jnp.bfloat16).astype(jnp.float32)

    load.wait()
    stores = []
    groups = out_weight_ref.shape[1] // width
    block = product_ref.shape[0] // groups
    shifted_ref[...] = jnp.zeros_like(shifted_ref)
    for first in range(8):
        shift = first * block % 8
        shifted_ref[0:8, :] = jnp.zeros((8, width), jnp.float32)
        shifted_ref[shift : shift + length, :] = conv_ref[...]
        shifted_ref[length + shift : length + 16, :] = jnp.zeros((16 - shift, width), jnp.float32)
        left = shifted_ref[...].astype(jnp.bfloat16)
        members = range(first, groups, 8)
        for pair in zip(members[::2], members[1::2]):
            right = jnp.concatenate([out_weight_ref[:, g * width : (g + 1) * width] for g in pair], axis=1)
            both = jnp.dot(left, right, preferred_element_type=jnp.float32)
            for place, g in enumerate(pair):
                base = g * block - shift
                rows = (g + 1) * block - (first + 1) * block % 8 - base
                product_ref[base : base + rows, :] = both[:rows, place * width : (place + 1) * width]
                store = pltpu.make_async_copy(
                    product_ref.at[pl.ds(base, rows), :], product_hbm.at[pl.ds(base, rows), :], store_sems.at[g]
                )
                store.start()
                stores.append(store)
    for store in stores:
        store.wait()


def per_device(query, key_proj, value, decay_rates, residues, skip_gain, out_weight):
    length, width = query.shape
    modes = decay_rates.shape[0]
    groups = out_weight.shape[1] // width
    block = length + 15
    shape = functools.partial(jax.ShapeDtypeStruct, dtype=jnp.float32)
    vmem = pl.BlockSpec(memory_space=pltpu.VMEM)
    chunk_states, end_state = pl.pallas_call(
        states_kernel,
        out_shape=(shape((chunks * modes, width)), shape((lax.axis_size("ctx"), modes, width))),
        scratch_shapes=[pltpu.VMEM((length, width), jnp.float32)],
    )(key_proj, value, decay_rates)
    ends = lax.all_to_all(end_state, "ctx", split_axis=0, concat_axis=0)
    local, weights = pl.pallas_call(
        local_kernel,
        out_shape=(shape((length, width)), shape((modes, width))),
        scratch_shapes=[pltpu.VMEM((chunks * modes, width), jnp.float32), pltpu.VMEM((length, width), jnp.float32)],
        cost_estimate=pl.CostEstimate(flops=70 * length * width, bytes_accessed=5 * length * width * 2, transcendentals=0),
    )(chunk_states, decay_rates, residues, skip_gain[None, :], query, key_proj, value)
    product = pl.pallas_call(
        product_kernel,
        out_shape=shape((groups * block, width)),
        in_specs=[pl.BlockSpec(memory_space=pltpu.SMEM)] + [vmem] * 5 + [pl.BlockSpec(memory_space=pl.ANY)],
        out_specs=pl.BlockSpec(memory_space=pl.ANY),
        scratch_shapes=[
            pltpu.VMEM((chunks * modes, width), jnp.float32),
            pltpu.VMEM((length, width), jnp.float32),
            pltpu.VMEM((length + 16, width), jnp.float32),
            pltpu.VMEM(out_weight.shape, jnp.bfloat16),
            pltpu.VMEM((groups * block, width), jnp.float32),
            pltpu.SemaphoreType.DMA,
            pltpu.SemaphoreType.DMA((groups,)),
        ],
        compiler_params=pltpu.CompilerParams(vmem_limit_bytes=60 * 1024 * 1024),
    )(lax.axis_index("ctx").reshape(1), ends, decay_rates, weights, query, local, out_weight)
    summed = lax.optimization_barrier(lax.psum_scatter(product, "tp", scatter_dimension=0, tiled=True))
    return (2.0 * summed[:length]).astype(jnp.bfloat16)


def solution(mesh):
    placed = (
        P("ctx", "tp"),
        P("ctx", "tp"),
        P("ctx", "tp"),
        P(None, "tp"),
        P(None, "tp"),
        P("tp"),
        P("tp", None),
    )
    return jax.shard_map(
        per_device, mesh=mesh, in_specs=placed, out_specs=P("ctx", "tp"), check_vma=False
    )
```

```python
import functools

import jax
import jax.numpy as jnp
from jax import lax
from jax.experimental import pallas as pl
from jax.experimental.pallas import tpu as pltpu
from jax.sharding import PartitionSpec as P

chunks = 8


def mode_rows(values, mode_count):
    return [jnp.broadcast_to(values[m : m + 1, :], (chunks, values.shape[1])) for m in range(mode_count)]


def one_minus_exp(x):
    series = jnp.ones_like(x)
    for k in range(9, 1, -1):
        series = 1.0 - x * series * (1.0 / k)
    return jnp.where(x < 0.25, x * series, 1.0 - jnp.exp(-x))


def states_kernel(key_ref, value_ref, rate_ref, chunk_ref, end_ref, signal_ref):
    modes = rate_ref.shape[0]
    steps = key_ref.shape[0] // chunks
    signal_ref[...] = key_ref[...].astype(jnp.float32) * value_ref[...].astype(jnp.float32)
    rates = rate_ref[...]
    decays = mode_rows(jnp.exp(-rates), modes)

    def step(t, states):
        x = signal_ref[pl.ds(t, chunks, stride=steps), :]
        return tuple(decays[m] * states[m] + x for m in range(modes))

    zero = jnp.zeros((chunks, rates.shape[1]), jnp.float32)
    states = lax.fori_loop(0, steps, step, (zero,) * modes, unroll=8)
    for m in range(modes):
        chunk_ref[pl.ds(m, chunks, stride=modes), :] = states[m]
    chunk_decay = jnp.exp(-float(steps) * rates)
    end = jnp.zeros_like(rates)
    for c in range(chunks):
        end = chunk_decay * end + chunk_ref[c * modes : (c + 1) * modes, :]
    end_ref[...] = jnp.broadcast_to(end[None], end_ref.shape)


def tree_sum(terms):
    while len(terms) > 1:
        terms = [terms[i] + terms[i + 1] for i in range(0, len(terms), 2)]
    return terms[0]


def local_kernel(
    chunk_ref, rate_ref, residue_ref, skip_ref, query_ref, key_ref, value_ref, local_ref, weight_ref, start_ref, signal_ref
):
    modes = rate_ref.shape[0]
    length, width = query_ref.shape
    steps = length // chunks
    rates = rate_ref[...]
    chunk_decay = jnp.exp(-float(steps) * rates)
    carry = jnp.zeros_like(rates)
    for c in range(chunks):
        rows = slice(c * modes, (c + 1) * modes)
        start_ref[rows, :] = carry
        carry = chunk_decay * carry + chunk_ref[rows, :]
    one_step = jnp.exp(-rates)
    weight = residue_ref[...] * jnp.sqrt(one_minus_exp(2.0 * rates))
    weight_ref[...] = weight * one_step
    decays = mode_rows(one_step, modes)
    weights = mode_rows(weight, modes)
    skip = jnp.broadcast_to(skip_ref[...], (chunks, width))
    signal_ref[...] = key_ref[...].astype(jnp.float32) * value_ref[...].astype(jnp.float32)

    def step(t, states):
        rows = pl.ds(t, chunks, stride=steps)
        x = signal_ref[rows, :]
        after = tuple(decays[m] * states[m] + x for m in range(modes))
        local_ref[rows, :] = tree_sum([weights[m] * after[m] for m in range(modes)]) + skip * x
        return after

    states = tuple(start_ref[pl.ds(m, chunks, stride=modes), :] for m in range(modes))
    lax.fori_loop(0, steps, step, states, unroll=4)


def product_kernel(
    index_ref,
    ends_ref,
    rate_ref,
    weight_ref,
    query_ref,
    local_ref,
    out_weight_ref,
    product_hbm,
    start_ref,
    conv_ref,
    shifted_ref,
    product_ref,
    store_sems,
):
    modes = rate_ref.shape[0]
    length, width = query_ref.shape
    steps = length // chunks
    index = index_ref[0]
    rates = rate_ref[...]
    block_decay = jnp.exp(-float(length) * rates)
    carry = jnp.zeros_like(rates)
    for d in range(ends_ref.shape[0]):
        carry = jnp.where(d < index, block_decay * carry + ends_ref[d], carry)
    chunk_decay = jnp.exp(-float(steps) * rates)
    carry = weight_ref[...] * carry
    for c in range(chunks):
        start_ref[c * modes : (c + 1) * modes, :] = carry
        carry = chunk_decay * carry
    decays = mode_rows(jnp.exp(-rates), modes)

    def step(t, tails):
        rows = pl.ds(t, chunks, stride=steps)
        conv_ref[rows, :] = local_ref[rows, :] + tree_sum(list(tails))
        return tuple(decays[m] * tails[m] for m in range(modes))

    tails = tuple(start_ref[pl.ds(m, chunks, stride=modes), :] for m in range(modes))
    lax.fori_loop(0, steps, step, tails, unroll=4)
    conv_ref[...] = ((0.5 * query_ref[...].astype(jnp.float32)) * conv_ref[...]).astype(jnp.bfloat16).astype(jnp.float32)

    stores = []
    groups = out_weight_ref.shape[1] // width
    block = product_ref.shape[0] // groups
    shifted_ref[...] = jnp.zeros_like(shifted_ref)
    for first in range(8):
        shift = first * block % 8
        shifted_ref[0:8, :] = jnp.zeros((8, width), jnp.float32)
        shifted_ref[shift : shift + length, :] = conv_ref[...]
        shifted_ref[length + shift : length + 16, :] = jnp.zeros((16 - shift, width), jnp.float32)
        left = shifted_ref[...].astype(jnp.bfloat16)
        members = range(first, groups, 8)
        for pair in zip(members[::2], members[1::2]):
            right = jnp.concatenate([out_weight_ref[:, g * width : (g + 1) * width] for g in pair], axis=1)
            both = jnp.dot(left, right, preferred_element_type=jnp.float32)
            for place, g in enumerate(pair):
                base = g * block - shift
                rows = (g + 1) * block - (first + 1) * block % 8 - base
                product_ref[base : base + rows, :] = both[:rows, place * width : (place + 1) * width]
                store = pltpu.make_async_copy(
                    product_ref.at[pl.ds(base, rows), :], product_hbm.at[pl.ds(base, rows), :], store_sems.at[g]
                )
                store.start()
                stores.append(store)
    for store in stores:
        store.wait()


def per_device(query, key_proj, value, decay_rates, residues, skip_gain, out_weight):
    length, width = query.shape
    modes = decay_rates.shape[0]
    groups = out_weight.shape[1] // width
    block = length + 15
    shape = functools.partial(jax.ShapeDtypeStruct, dtype=jnp.float32)
    vmem = pl.BlockSpec(memory_space=pltpu.VMEM)
    chunk_states, end_state = pl.pallas_call(
        states_kernel,
        out_shape=(shape((chunks * modes, width)), shape((lax.axis_size("ctx"), modes, width))),
        scratch_shapes=[pltpu.VMEM((length, width), jnp.float32)],
    )(key_proj, value, decay_rates)
    ends = lax.all_to_all(end_state, "ctx", split_axis=0, concat_axis=0)
    local, weights = pl.pallas_call(
        local_kernel,
        out_shape=(shape((length, width)), shape((modes, width))),
        scratch_shapes=[pltpu.VMEM((chunks * modes, width), jnp.float32), pltpu.VMEM((length, width), jnp.float32)],
        cost_estimate=pl.CostEstimate(flops=70 * length * width, bytes_accessed=5 * length * width * 2, transcendentals=0),
    )(chunk_states, decay_rates, residues, skip_gain[None, :], query, key_proj, value)
    product = pl.pallas_call(
        product_kernel,
        out_shape=shape((groups * block, width)),
        in_specs=[pl.BlockSpec(memory_space=pltpu.SMEM)] + [vmem] * 6,
        out_specs=pl.BlockSpec(memory_space=pl.ANY),
        scratch_shapes=[
            pltpu.VMEM((chunks * modes, width), jnp.float32),
            pltpu.VMEM((length, width), jnp.float32),
            pltpu.VMEM((length + 16, width), jnp.float32),
            pltpu.VMEM((groups * block, width), jnp.float32),
            pltpu.SemaphoreType.DMA((groups,)),
        ],
        compiler_params=pltpu.CompilerParams(vmem_limit_bytes=60 * 1024 * 1024),
    )(lax.axis_index("ctx").reshape(1), ends, decay_rates, weights, query, local, out_weight)
    summed = lax.optimization_barrier(lax.psum_scatter(product, "tp", scatter_dimension=0, tiled=True))
    return (2.0 * summed[:length]).astype(jnp.bfloat16)


def solution(mesh):
    placed = (
        P("ctx", "tp"),
        P("ctx", "tp"),
        P("ctx", "tp"),
        P(None, "tp"),
        P(None, "tp"),
        P("tp"),
        P("tp", None),
    )
    return jax.shard_map(
        per_device, mesh=mesh, in_specs=placed, out_specs=P("ctx", "tp"), check_vma=False
    )
```

```python
import functools

import jax
import jax.numpy as jnp
from jax import lax
from jax.experimental import pallas as pl
from jax.experimental.pallas import tpu as pltpu
from jax.sharding import PartitionSpec as P

chunks = 8


def mode_rows(values, mode_count):
    return [jnp.broadcast_to(values[m : m + 1, :], (chunks, values.shape[1])) for m in range(mode_count)]


def one_minus_exp(x):
    series = jnp.ones_like(x)
    for k in range(9, 1, -1):
        series = 1.0 - x * series * (1.0 / k)
    return jnp.where(x < 0.25, x * series, 1.0 - jnp.exp(-x))


def states_kernel(key_ref, value_ref, rate_ref, chunk_ref, end_ref, signal_ref):
    modes = rate_ref.shape[0]
    steps = key_ref.shape[0] // chunks
    signal_ref[...] = key_ref[...].astype(jnp.float32) * value_ref[...].astype(jnp.float32)
    rates = rate_ref[...]
    decays = mode_rows(jnp.exp(-rates), modes)

    def step(t, states):
        x = signal_ref[pl.ds(t, chunks, stride=steps), :]
        return tuple(decays[m] * states[m] + x for m in range(modes))

    zero = jnp.zeros((chunks, rates.shape[1]), jnp.float32)
    states = lax.fori_loop(0, steps, step, (zero,) * modes, unroll=8)
    for m in range(modes):
        chunk_ref[pl.ds(m, chunks, stride=modes), :] = states[m]
    chunk_decay = jnp.exp(-float(steps) * rates)
    end = jnp.zeros_like(rates)
    for c in range(chunks):
        end = chunk_decay * end + chunk_ref[c * modes : (c + 1) * modes, :]
    end_ref[...] = jnp.broadcast_to(end[None], end_ref.shape)


def tree_sum(terms):
    while len(terms) > 1:
        terms = [terms[i] + terms[i + 1] for i in range(0, len(terms), 2)]
    return terms[0]


def local_kernel(
    chunk_ref, rate_ref, residue_ref, skip_ref, query_ref, key_ref, value_ref, local_ref, weight_ref, start_ref, signal_ref
):
    modes = rate_ref.shape[0]
    length, width = query_ref.shape
    steps = length // chunks
    rates = rate_ref[...]
    chunk_decay = jnp.exp(-float(steps) * rates)
    carry = jnp.zeros_like(rates)
    for c in range(chunks):
        rows = slice(c * modes, (c + 1) * modes)
        start_ref[rows, :] = carry
        carry = chunk_decay * carry + chunk_ref[rows, :]
    one_step = jnp.exp(-rates)
    weight = residue_ref[...] * jnp.sqrt(one_minus_exp(2.0 * rates))
    weight_ref[...] = weight * one_step
    decays = mode_rows(one_step, modes)
    weights = mode_rows(weight, modes)
    skip = jnp.broadcast_to(skip_ref[...], (chunks, width))
    signal_ref[...] = key_ref[...].astype(jnp.float32) * value_ref[...].astype(jnp.float32)

    def step(t, states):
        rows = pl.ds(t, chunks, stride=steps)
        x = signal_ref[rows, :]
        after = tuple(decays[m] * states[m] + x for m in range(modes))
        local_ref[rows, :] = tree_sum([weights[m] * after[m] for m in range(modes)]) + skip * x
        return after

    states = tuple(start_ref[pl.ds(m, chunks, stride=modes), :] for m in range(modes))
    lax.fori_loop(0, steps, step, states, unroll=4)


def product_kernel(
    index_ref,
    ends_ref,
    rate_ref,
    weight_ref,
    query_ref,
    local_ref,
    out_weight_ref,
    product_hbm,
    start_ref,
    conv_ref,
    shifted_ref,
    product_ref,
    store_sems,
):
    modes = rate_ref.shape[0]
    length, width = query_ref.shape
    steps = length // chunks
    index = index_ref[0]
    rates = rate_ref[...]
    block_decay = jnp.exp(-float(length) * rates)
    carry = jnp.zeros_like(rates)
    for d in range(ends_ref.shape[0]):
        carry = jnp.where(d < index, block_decay * carry + ends_ref[d], carry)
    chunk_decay = jnp.exp(-float(steps) * rates)
    carry = weight_ref[...] * carry
    for c in range(chunks):
        start_ref[c * modes : (c + 1) * modes, :] = carry
        carry = chunk_decay * carry
    decays = mode_rows(jnp.exp(-rates), modes)

    def step(t, tails):
        rows = pl.ds(t, chunks, stride=steps)
        conv_ref[rows, :] = local_ref[rows, :] + tree_sum(list(tails))
        return tuple(decays[m] * tails[m] for m in range(modes))

    tails = tuple(start_ref[pl.ds(m, chunks, stride=modes), :] for m in range(modes))
    lax.fori_loop(0, steps, step, tails, unroll=4)
    conv_ref[...] = ((0.5 * query_ref[...].astype(jnp.float32)) * conv_ref[...]).astype(jnp.bfloat16).astype(jnp.float32)

    stores = []
    groups = out_weight_ref.shape[1] // width
    block = product_ref.shape[0] // groups
    half = length // 2
    for first in range(8):
        shift = first * block % 8
        lefts = []
        for part in range(2):
            shifted_ref[0:8, :] = jnp.zeros((8, width), jnp.float32)
            shifted_ref[shift : shift + half, :] = conv_ref[part * half : (part + 1) * half, :]
            shifted_ref[half + shift : half + 16, :] = jnp.zeros((16 - shift, width), jnp.float32)
            lefts.append(shifted_ref[...].astype(jnp.bfloat16))
        members = range(first, groups, 8)
        for pair in zip(members[::2], members[1::2]):
            right = jnp.concatenate([out_weight_ref[:, g * width : (g + 1) * width] for g in pair], axis=1)
            both = [jnp.dot(left, right, preferred_element_type=jnp.float32) for left in lefts]
            for place, g in enumerate(pair):
                base = g * block - shift
                rows = (g + 1) * block - (first + 1) * block % 8 - base
                for part in range(2):
                    product_ref[base : base + rows, part * width : (part + 1) * width] = both[part][
                        :rows, place * width : (place + 1) * width
                    ]
                store = pltpu.make_async_copy(
                    product_ref.at[pl.ds(base, rows), :], product_hbm.at[pl.ds(base, rows), :], store_sems.at[g]
                )
                store.start()
                stores.append(store)
    for store in stores:
        store.wait()


def per_device(query, key_proj, value, decay_rates, residues, skip_gain, out_weight):
    length, width = query.shape
    modes = decay_rates.shape[0]
    groups = out_weight.shape[1] // width
    half = length // 2
    block = half + 7
    shape = functools.partial(jax.ShapeDtypeStruct, dtype=jnp.float32)
    vmem = pl.BlockSpec(memory_space=pltpu.VMEM)
    chunk_states, end_state = pl.pallas_call(
        states_kernel,
        out_shape=(shape((chunks * modes, width)), shape((lax.axis_size("ctx"), modes, width))),
        scratch_shapes=[pltpu.VMEM((length, width), jnp.float32)],
    )(key_proj, value, decay_rates)
    ends = lax.all_to_all(end_state, "ctx", split_axis=0, concat_axis=0)
    local, weights = pl.pallas_call(
        local_kernel,
        out_shape=(shape((length, width)), shape((modes, width))),
        scratch_shapes=[pltpu.VMEM((chunks * modes, width), jnp.float32), pltpu.VMEM((length, width), jnp.float32)],
        cost_estimate=pl.CostEstimate(flops=70 * length * width, bytes_accessed=5 * length * width * 2, transcendentals=0),
    )(chunk_states, decay_rates, residues, skip_gain[None, :], query, key_proj, value)
    product = pl.pallas_call(
        product_kernel,
        out_shape=shape((groups * block, 2 * width)),
        in_specs=[pl.BlockSpec(memory_space=pltpu.SMEM)] + [vmem] * 6,
        out_specs=pl.BlockSpec(memory_space=pl.ANY),
        scratch_shapes=[
            pltpu.VMEM((chunks * modes, width), jnp.float32),
            pltpu.VMEM((length, width), jnp.float32),
            pltpu.VMEM((half + 16, width), jnp.float32),
            pltpu.VMEM((groups * block, 2 * width), jnp.float32),
            pltpu.SemaphoreType.DMA((groups,)),
        ],
        compiler_params=pltpu.CompilerParams(vmem_limit_bytes=60 * 1024 * 1024),
    )(lax.axis_index("ctx").reshape(1), ends, decay_rates, weights, query, local, out_weight)
    summed = lax.optimization_barrier(lax.psum_scatter(product, "tp", scatter_dimension=0, tiled=True))
    joined = jnp.concatenate([summed[:half, :width], summed[:half, width:]])
    return (2.0 * joined).astype(jnp.bfloat16)


def solution(mesh):
    placed = (
        P("ctx", "tp"),
        P("ctx", "tp"),
        P("ctx", "tp"),
        P(None, "tp"),
        P(None, "tp"),
        P("tp"),
        P("tp", None),
    )
    return jax.shard_map(
        per_device, mesh=mesh, in_specs=placed, out_specs=P("ctx", "tp"), check_vma=False
    )
```
